256 devices in a mesh: dp: 8 (over x, z_lo), expert: 32 (over z_hi, y, core).
Axes of the slice: x: 4, y: 4, z: 8 (z_hi: 4, z_lo: 2; z = z_hi * 2 + z_lo), core: 2. Of those that a mesh axis runs over, the one named last changes fastest.
Arguments:
- tokens: bfloat16 [32768, 4096], P(('dp', 'expert')), may hold values from -6 to 6
- cotangent: bfloat16 [32768, 4096], P(('dp', 'expert')), may hold values from -1.5 to 1.5
- expert_ids: int32 [32768, 2], P(('dp', 'expert')), may hold values from 0 to 31, all different within a row; in each aligned block of 128 rows (0 to 127, 128 to 255, ...) at most 8 rows name the same one
- gate_vals: bfloat16 [32768, 2], P(('dp', 'expert')), may hold values from 0.099609375 to 1
- partner: int32 [32], replicated, may hold values from 0 to 31, as said below
- gate_weight: bfloat16 [32, 4096, 512], P('expert', 'dp'), may hold values from -0.09375 to 0.09375
- up_weight: bfloat16 [32, 4096, 512], P('expert', 'dp'), may hold values from -0.09375 to 0.09375
- down_weight_t: bfloat16 [32, 4096, 512], P('expert', 'dp'), may hold values from -0.25 to 0.25
Outputs:
- grad_tokens: bfloat16 [32768, 4096], P(('dp', 'expert'))
- grad_gates: bfloat16 [32768, 2], P(('dp', 'expert'))
- grad_gate_weight: bfloat16 [32, 4096, 512], P('expert', 'dp')
- grad_up_weight: bfloat16 [32, 4096, 512], P('expert', 'dp')
- grad_down_weight_t: bfloat16 [32, 4096, 512], P('expert', 'dp')
The draws below stay inside these ranges and needn't reach their ends.
Inputs may be any that keep to these rules, and one draw needn't show every extreme that they name: `expert_ids`: among the 128 tokens of each device every expert is named in exactly 8 slots, and a token's 2 experts differ. partner[i] = i XOR m for one power of two m below 32, the same m for every i.
All inputs are finite; a program needn't handle non-finite values.
Results may differ from the reference program's by a relative error of at most 0.024.
Values may be sent and summed in bfloat16 or wider, within the bound.
No kernel may reach another device: no remote copies, remote signals or barrier semaphores. Data moves between devices by JAX's collectives and lax.ppermute only.
A program may use at most 128 MiB of HBM per device.

```python
import math
import jax
import jax.numpy as jnp
import numpy as np
from jax import lax

D = 4096
HIDDEN_SIZE = 512
TOP = 2
TOK_DEV = 128
EXPERTS = 32
CAP = 8
GROUP_TOK = 4096
TOKENS = 32768
N_DP = 8


def draw_partner(key, part):
    key = jax.random.fold_in(key, 7)
    count = EXPERTS.bit_length() - 1
    chosen_bit = jax.random.randint(key, (), 0, count)
    flip_mask = jnp.left_shift(jnp.int32(1), chosen_bit.astype(jnp.int32))
    return jnp.bitwise_xor(jnp.arange(EXPERTS, dtype=jnp.int32), flip_mask)


def block_scale(key, extent, shards, smallest, top_value):
    def one(position, parts):
        heights = jax.random.uniform(jax.random.fold_in(jax.random.fold_in(key, 6), position), (parts,), jnp.float32, smallest / len(shards), top_value / len(shards))
        return jnp.repeat(jnp.exp(heights), extent[position] // parts).reshape((-1,) + (1,) * (len(extent) - position - 1))

    loudness = one(*shards[0])
    for cut in shards[1:]:
        loudness = loudness * one(*cut)
    return loudness


def shared_out(key, own, number, rows, number_of, top, reach, slope):
    order = jax.random.permutation(key, number_of)
    crowded, common = portions_of(number_of, rows * top, reach, slope, True), portions_of(number_of, rows * top, reach, slope, False)
    places = jnp.arange(number_of)

    def named(lengths, offset_by):
        used = int((lengths > 0).sum())
        fixed = max(1, used // 4)
        shifted = fixed + (places - fixed + offset_by * (used - fixed)) % max(1, number_of - fixed)
        return jnp.zeros((number_of,), jnp.int32).at[order[jnp.where(places < fixed, places, shifted)]].set(jnp.asarray(lengths, jnp.int32))

    lengths = jnp.where(number % 4 == 0, named(crowded, number // 4), named(common, number - number // 4 - 1))
    mixed = jax.random.permutation(jax.random.fold_in(own, 3), number_of)
    source_of, receiver = mixed[0:number_of // 2 * 2:2], mixed[1:number_of // 2 * 2:2]
    margin = jnp.minimum(lengths[source_of] - 1, reach - lengths[receiver]) // 2
    margin = jnp.where((source_of == order[0]) | (receiver == order[0]) | (lengths[receiver] == 0), 0, jnp.maximum(margin, 0))
    shifted = jax.random.randint(jax.random.fold_in(own, 4), (number_of // 2,), 0, 1 << 20) % (margin + 1)
    lengths = lengths.at[source_of].add(-shifted).at[receiver].add(shifted)
    members = jnp.searchsorted(jnp.cumsum(lengths), jnp.arange(rows * top), side="right").astype(jnp.int32)
    grid = members.reshape(top, rows).T
    grid = grid[jax.random.permutation(jax.random.fold_in(own, 1), rows)]
    offset_by = jax.random.randint(jax.random.fold_in(own, 2), (rows, 1), 0, top)
    return jnp.take_along_axis(grid, (jnp.arange(top)[None, :] + offset_by) % top, axis=1)


def portions_of(number_of, total, most, slope, full):
    weights = [(1 << 20) // math.isqrt(grade ** slope) + 1 for grade in range(1, number_of + 1)]
    largest = most if full else min(most, max(-(-total // number_of), total * weights[0] // sum(weights)))
    least = 1 if total - largest >= number_of - 1 else 0
    holding, spare = [largest] + [least] * (number_of - 1), total - largest - least * (number_of - 1)
    while spare > 0:
        candidates = [i for i in range(1, number_of) if holding[i] < largest] or [i for i in range(1, number_of) if holding[i] < most]
        pool, left = sum([weights[i] for i in candidates]), spare
        for i in candidates:
            extra = min(most - holding[i], max(1, left * weights[i] // pool), spare)
            holding[i] = holding[i] + extra
            spare = spare - extra
    return np.array(holding)


def bell_draw(rng, dims, deviation, reach, shards=(), held_as=jnp.bfloat16):
    result = deviation * jax.random.normal(rng, dims, jnp.float32)
    if shards:
        result = result * block_scale(rng, dims, shards, -0.22, 0.18)
    return jnp.clip(result, -reach, reach).astype(held_as)


def setup_inputs(seed: int = 0) -> dict:
    keys = jax.random.split(jax.random.key(seed), 9)
    tokens = bell_draw(keys[0], (TOKENS, D), 1.0, 6.0, ((0, 256),))
    cotangent = bell_draw(keys[1], (TOKENS, D), 0.25, 1.5, ((0, 256),))
    expert_ids_keys = jax.random.split(jax.random.fold_in(keys[2], 1), TOKENS // TOK_DEV)
    expert_ids_turns = jax.random.permutation(jax.random.fold_in(keys[2], 3), TOKENS // TOK_DEV)
    expert_ids = jax.vmap(lambda own, number: shared_out(jax.random.fold_in(keys[2], 2), own, number, TOK_DEV, EXPERTS, TOP, CAP, 0))(expert_ids_keys, expert_ids_turns).reshape((TOKENS, TOP))
    gate_vals = jnp.clip(0.099609375 + 0.9003906 * jax.random.uniform(keys[3], (TOKENS, TOP), jnp.float32) ** block_scale(keys[3], (TOKENS, TOP), ((0, 256),), -0.2, 0.2), 0.099609375, 1.0).astype(jnp.bfloat16)
    partner = draw_partner(jax.random.fold_in(keys[8], 71), 0)
    gate_weight = bell_draw(keys[5], (EXPERTS, D, HIDDEN_SIZE), D ** -0.5, 0.09375, ((0, 32), (1, 8)))
    up_weight = bell_draw(keys[6], (EXPERTS, D, HIDDEN_SIZE), D ** -0.5, 0.09375, ((0, 32), (1, 8)))
    down_weight_t = bell_draw(keys[7], (EXPERTS, D, HIDDEN_SIZE), HIDDEN_SIZE ** -0.5, 0.25, ((0, 32), (1, 8)))
    return dict(tokens=tokens, cotangent=cotangent, expert_ids=expert_ids, gate_vals=gate_vals, partner=partner, gate_weight=gate_weight, up_weight=up_weight, down_weight_t=down_weight_t)


def reference(tokens, cotangent, expert_ids, gate_vals, partner, gate_weight, up_weight, down_weight_t):
    groups = N_DP
    slots_group = TOP * GROUP_TOK
    picked = slots_group // EXPERTS
    group_ids = expert_ids.reshape(groups, slots_group)
    flat_gates = gate_vals.reshape(-1)
    base = (jnp.arange(groups, dtype=jnp.int32) * slots_group)[:, None]

    def one_expert(carry, expert):
        input_acc, gate_acc = carry
        chosen = jnp.argsort((group_ids != expert).astype(jnp.int32), axis=1, stable=True)[:, :picked].astype(jnp.int32)
        slot = (base + chosen).reshape(-1)
        token = (slot // TOP).astype(jnp.int32)
        rows = tokens[token].astype(jnp.float32).reshape(groups, picked, D)
        grads_in = cotangent[token].astype(jnp.float32).reshape(groups, picked, D)
        gates = flat_gates[slot].astype(jnp.float32).reshape(groups, picked, 1)
        w_gate = gate_weight[expert].astype(jnp.float32)
        w_up = up_weight[expert].astype(jnp.float32)
        w_down = down_weight_t[expert].astype(jnp.float32)
        pre_gate = jnp.einsum("grd,df->grf", rows, w_gate)
        pre_up = jnp.einsum("grd,df->grf", rows, w_up)
        sig = jax.nn.sigmoid(pre_gate)
        silu_val = pre_gate * sig
        act = (silu_val * pre_up).astype(jnp.bfloat16).astype(jnp.float32)
        expert_out = jnp.einsum("grf,df->grd", act, w_down)
        grad_gate_slot = jnp.sum(expert_out * grads_in, axis=2).astype(jnp.bfloat16).astype(jnp.float32)
        slot_grad = (gates * grads_in).astype(jnp.bfloat16).astype(jnp.float32)
        grad_act = jnp.einsum("grd,df->grf", slot_grad, w_down)
        grad_pre_gate = (grad_act * pre_up * sig * (1.0 + pre_gate * (1.0 - sig))).astype(jnp.bfloat16).astype(jnp.float32)
        grad_pre_up = (grad_act * silu_val).astype(jnp.bfloat16).astype(jnp.float32)
        slot_input = jnp.einsum("grf,df->grd", grad_pre_gate, w_gate) + jnp.einsum("grf,df->grd", grad_pre_up, w_up)
        slot_input = slot_input.astype(jnp.bfloat16).astype(jnp.float32)
        input_acc = input_acc.at[token].add(slot_input.reshape(-1, D))
        gate_acc = gate_acc.at[slot].set(grad_gate_slot.reshape(-1))
        part_gate = jnp.einsum("grd,grf->gdf", rows, grad_pre_gate).astype(jnp.bfloat16).astype(jnp.float32)
        part_up = jnp.einsum("grd,grf->gdf", rows, grad_pre_up).astype(jnp.bfloat16).astype(jnp.float32)
        part_down = jnp.einsum("grd,grf->gdf", slot_grad, act).astype(jnp.bfloat16).astype(jnp.float32)
        total_gate = jnp.sum(part_gate, axis=0).astype(jnp.bfloat16)
        total_up = jnp.sum(part_up, axis=0).astype(jnp.bfloat16)
        total_down = jnp.sum(part_down, axis=0).astype(jnp.bfloat16)
        return (input_acc, gate_acc), (total_gate, total_up, total_down)

    start = (jnp.zeros((TOKENS, D), jnp.float32), jnp.zeros((TOKENS * TOP,), jnp.float32))
    (input_acc, gate_acc), (all_gate, all_up, all_down) = lax.scan(one_expert, start, jnp.arange(EXPERTS, dtype=jnp.int32))
    grad_tokens = input_acc.astype(jnp.bfloat16)
    grad_gates = gate_acc.reshape(TOKENS, TOP).astype(jnp.bfloat16)
    owner = partner.astype(jnp.int32)
    return grad_tokens, grad_gates, all_gate[owner], all_up[owner], all_down[owner]
```

```python
import jax
import jax.numpy as jnp
from jax import lax
from jax.sharding import Mesh, PartitionSpec as P

BF, F32 = jnp.bfloat16, jnp.float32
X, ZL = 4, 2
EXTRA = 128


def moved(values, flip_mask, count):
    bits = count.bit_length() - 1
    which = jnp.int32(0)
    for bit in range(bits):
        which = which + jnp.where(flip_mask == 1 << bit, bit, 0).astype(jnp.int32)

    def flipper(bit):
        pairs = [(i, i ^ 1 << bit) for i in range(count)]
        return lambda v: lax.ppermute(v, "expert", pairs)

    return lax.switch(which, [flipper(bit) for bit in range(bits)], values)


def swap(value):
    return lax.ppermute(value, "zl", [(0, 1), (1, 0)])


def dot(a, b, dims=((1,), (0,))):
    return lax.dot_general(a, b, (dims, ((), ())), preferred_element_type=F32)


def shards(tokens, cotangent, expert_ids, gate_vals, partner, gate_weight, up_weight, down_weight_t):
    experts = lax.axis_size("expert")
    zl = lax.axis_index("zl")
    tok_rows, width = tokens.shape
    hidden = gate_weight.shape[2]
    block = gate_weight.shape[1]
    top = expert_ids.shape[1]
    slots = tok_rows * top
    cap = slots // experts
    part = X * block
    flip_mask = partner[0]

    stacked = jnp.concatenate((gate_weight[0], up_weight[0], down_weight_t[0]), axis=1)
    whole = lax.all_gather(moved(stacked, flip_mask, experts), "x", axis=0, tiled=True)
    w_pair, w_down = whole[:, : 2 * hidden], whole[:, 2 * hidden :]

    dest = jnp.bitwise_xor(expert_ids, flip_mask)
    flat = dest.reshape(-1)
    order = jnp.arange(slots, dtype=jnp.int32)
    earlier = (flat[:, None] == flat[None, :]) & (order[None, :] < order[:, None])
    rank = jnp.sum(earlier.astype(jnp.int32), axis=1)
    place = (flat * cap + rank).reshape(tok_rows, top)
    picks = [(order[:, None] == place[None, :, k]) for k in range(top)]
    pick = (picks[0] | picks[1]).astype(BF)
    gates = gate_vals.astype(F32)
    slot_gate = sum(jnp.sum(jnp.where(picks[k], gates[None, :, k], 0.0), axis=1) for k in range(top))

    def halves(array):
        parts = array.reshape(tok_rows, X, ZL, block)
        return [parts[:, :, z].reshape(tok_rows, part) for z in range(ZL)]

    send_rows = jnp.stack([dot(pick, h).astype(BF) for h in halves(tokens)])
    send_grads = jnp.stack([(slot_gate[:, None] * dot(pick, h)).astype(BF) for h in halves(cotangent)])

    def exchange(value):
        value = value.reshape(ZL * experts, cap, -1)
        return lax.all_to_all(value, ("zl", "expert"), 0, 0, tiled=True).reshape(ZL * slots, -1)

    rows = exchange(send_rows)
    grads_in = exchange(send_grads)

    def summed(partial):
        partial = partial.reshape(ZL, slots, -1)
        other = swap(lax.dynamic_index_in_dim(partial, 1 - zl, keepdims=False).astype(BF))
        return lax.dynamic_index_in_dim(partial, zl, keepdims=False) + other.astype(F32)

    def both(value):
        other = swap(value)
        first = zl == 0
        return jnp.concatenate((jnp.where(first, value, other), jnp.where(first, other, value)))

    pre = summed(dot(rows, w_pair))
    pre_gate, pre_up = pre[:, :hidden], pre[:, hidden:]
    sig = jax.nn.sigmoid(pre_gate)
    silu_val = pre_gate * sig
    act = (silu_val * pre_up).astype(BF)
    act_all = both(act)

    grad_act = summed(dot(grads_in, w_down))
    grad_pre_gate = (grad_act * pre_up * sig * (1.0 + pre_gate * (1.0 - sig))).astype(BF)
    grad_pre_up = (grad_act * silu_val).astype(BF)
    pair_all = both(jnp.concatenate((grad_pre_gate, grad_pre_up), axis=1))
    scaled = jnp.sum(act.astype(F32) * grad_act, axis=1, keepdims=True)

    down_part = dot(grads_in, act_all, ((0,), (0,))).astype(BF)
    pair_part = dot(rows, pair_all, ((0,), (0,))).astype(BF)
    grad_down = lax.psum_scatter(down_part, "x", scatter_dimension=0, tiled=True)
    grad_pair = lax.psum_scatter(pair_part, "x", scatter_dimension=0, tiled=True)

    slot_input = dot(pair_all, w_pair, ((1,), (1,))).astype(BF)
    high = scaled.astype(BF)
    low = (scaled - high.astype(F32)).astype(BF)
    lane = lax.broadcasted_iota(jnp.int32, (slots, EXTRA), 1)
    extra = jnp.where(lane == 0, high, jnp.where(lane == 1, low, 0))
    side = lax.broadcasted_iota(jnp.int32, (ZL, 1, 1), 0) == zl
    extra = jnp.where(side, extra[None], 0).reshape(ZL * slots, EXTRA)
    back = exchange(jnp.concatenate((slot_input, extra), axis=1)).reshape(ZL, slots, part + EXTRA)

    outs = [dot(pick, back[z, :, :part], ((0,), (0,))).astype(BF).reshape(tok_rows, X, block) for z in range(ZL)]
    grad_tokens = jnp.stack(outs, axis=2).reshape(tok_rows, width)
    tail = back[:, :, part : part + 2].astype(F32)
    total = jnp.sum(tail, axis=(0, 2))
    per_slot = jnp.stack([jnp.sum(jnp.where(picks[k], total[:, None], 0.0), axis=0) for k in range(top)], axis=1)
    grad_gates = (per_slot / gates).astype(BF)
    return (
        grad_tokens,
        grad_gates,
        grad_pair[None, :, :hidden],
        grad_pair[None, :, hidden:],
        grad_down[None],
    )


def solution(mesh):
    split = Mesh(mesh.devices.reshape(X, ZL, -1), ("x", "zl", "expert"))
    every = ("x", "zl", "expert")
    tok = P(every, None)
    weight = P("expert", ("x", "zl"), None)
    return jax.shard_map(
        shards,
        mesh=split,
        in_specs=(tok, tok, tok, tok, P(), weight, weight, weight),
        out_specs=(tok, tok, weight, weight, weight),
        check_vma=False,
    )
```

```python
from functools import partial

import jax
import jax.numpy as jnp
from jax import lax
from jax.experimental import pallas as pl
from jax.experimental.pallas import tpu as pltpu
from jax.sharding import Mesh, PartitionSpec as P

BF, F32 = jnp.bfloat16, jnp.float32
X, ZL = 4, 2
EXTRA = 128
TILE = 256


def dot(a, b, dims=((1,), (0,))):
    return lax.dot_general(a, b, (dims, ((), ())), preferred_element_type=F32)


def call(kernel, outs, *args, scalars=0, loaded=0):
    spaces = [pltpu.SMEM] * scalars + [pltpu.VMEM] * (len(args) - scalars - loaded) + [pl.ANY] * loaded
    scratch = []
    if loaded:
        scratch = [pltpu.VMEM((loaded, *args[-1].shape), args[-1].dtype), pltpu.SemaphoreType.DMA((loaded,))]
    return pl.pallas_call(
        kernel,
        out_shape=[jax.ShapeDtypeStruct(shape, dtype) for shape, dtype in outs],
        in_specs=[pl.BlockSpec(memory_space=space) for space in spaces],
        out_specs=[pl.BlockSpec(memory_space=pltpu.VMEM)] * len(outs),
        scratch_shapes=scratch,
        compiler_params=pltpu.CompilerParams(vmem_limit_bytes=32 << 20),
    )(*args)


def picks_of(experts, ids):
    top, tok_rows = ids.shape
    slots = top * tok_rows
    cap = slots // experts
    expert = lax.broadcasted_iota(jnp.int32, (experts, tok_rows), 0)
    before = lax.broadcasted_iota(jnp.int32, (tok_rows, tok_rows), 0)
    before = (before < lax.broadcasted_iota(jnp.int32, (tok_rows, tok_rows), 1)).astype(BF)
    place = lax.broadcasted_iota(jnp.int32, (slots, tok_rows), 0)
    taken = jnp.zeros((experts, 1), F32)
    picks = []
    for k in range(top):
        named = expert == ids[k : k + 1]
        ones = jnp.where(named, 1.0, 0.0)
        rank = jnp.sum(jnp.where(named, dot(ones.astype(BF), before) + taken, 0.0), axis=0, keepdims=True)
        taken = taken + jnp.sum(ones, axis=1, keepdims=True)
        picks.append(place == ids[k : k + 1] * cap + rank.astype(jnp.int32))
    return picks


def gathered(picks, at, source_ref, block, scale, store):
    pick = jnp.where(picks[0] | picks[1], 1.0, 0.0).astype(BF)
    for z in range(ZL):
        for s in range(X):
            column = pl.multiple_of((lax.rem(at + s, X) * ZL + z) * block, block)
            value = dot(pick, source_ref[:, pl.ds(column, block)])
            store(z, s, (value if scale is None else value * scale).astype(BF))


def rows_kernel(experts, at_ref, ids_ref, tokens_ref, out_ref):
    block = tokens_ref.shape[1] // (X * ZL)
    picks = picks_of(experts, ids_ref[...])

    def store(z, s, value):
        out_ref[z, :, s * block : (s + 1) * block] = value

    gathered(picks, at_ref[0], tokens_ref, block, None, store)


def grads_kernel(experts, at_ref, ids_ref, gates_ref, cotangent_ref, out_ref):
    block = cotangent_ref.shape[1] // (X * ZL)
    picks = picks_of(experts, ids_ref[...])
    scale = sum(jnp.sum(jnp.where(p, gates_ref[k : k + 1], 0.0), axis=1, keepdims=True) for k, p in enumerate(picks))

    def store(z, s, value):
        out_ref[z, :, s * block : (s + 1) * block] = value

    gathered(picks, at_ref[0], cotangent_ref, block, scale, store)


def collect_kernel(experts, at_ref, ids_ref, gates_ref, back_ref, tokens_ref, gates_out_ref):
    block = tokens_ref.shape[1] // (X * ZL)
    picks = picks_of(experts, ids_ref[...])
    pick = jnp.where(picks[0] | picks[1], 1.0, 0.0).astype(BF)
    for z in range(ZL):
        for s in range(X):
            column = pl.multiple_of((lax.rem(at_ref[0] + s, X) * ZL + z) * block, block)
            value = dot(pick, back_ref[z, :, s * block : (s + 1) * block], ((0,), (0,)))
            tokens_ref[:, pl.ds(column, block)] = value.astype(BF)
    total = jnp.sum(back_ref[0, :, X * block :].astype(F32), axis=1, keepdims=True)
    sums = [jnp.sum(jnp.where(p, total, 0.0), axis=0, keepdims=True) for p in picks]
    gates_out_ref[...] = jnp.concatenate(sums, axis=0) / gates_ref[...]


def forward_kernel(rows_ref, *refs):
    *sources, own_ref, sent_ref, weights, sems = refs
    rows, columns = own_ref.shape
    count, block, hidden = weights.shape
    copies = [pltpu.make_async_copy(sources[i], weights.at[i], sems.at[i]) for i in range(count)]
    for copy in copies:
        copy.start()
    for i in range(count // X):
        for copy in copies[i * X : (i + 1) * X]:
            copy.wait()
        for m in range(0, rows, TILE):
            for n in range(0, hidden, TILE):
                total = None
                for s in range(X):
                    weight = weights[i * X + s, :, n : n + TILE]
                    term = dot(rows_ref[m : m + TILE, s * block : (s + 1) * block], weight)
                    total = term if total is None else total + term
                at = i * hidden + n
                own_ref[m : m + TILE, at : at + TILE] = total
                sent_ref[m : m + TILE, at : at + TILE] = total.astype(BF)


def back_kernel(own_ref, other_ref, slope_ref, silu_ref, act_ref, *refs):
    *weights, gate_ref, up_ref, back_ref = refs
    rows, hidden = own_ref.shape
    block = weights[0].shape[0]
    for m in range(0, rows, TILE):
        at = slice(m, m + TILE)
        grad_act = own_ref[at] + other_ref[at].astype(F32)
        gate_ref[at] = (grad_act * slope_ref[at]).astype(BF)
        up_ref[at] = (grad_act * silu_ref[at]).astype(BF)
        scaled = jnp.sum(act_ref[at].astype(F32) * grad_act, axis=1, keepdims=True)
        high = scaled.astype(BF).astype(F32)
        lane = lax.broadcasted_iota(jnp.int32, (TILE, EXTRA), 1)
        extra = jnp.where(lane == 0, high, jnp.where(lane == 1, scaled - high, 0.0))
        back_ref[at, X * block :] = extra.astype(BF)
        for s in range(X):
            for n in range(0, block, TILE):
                value = dot(gate_ref[at], weights[s][n : n + TILE], ((1,), (1,)))
                value = value + dot(up_ref[at], weights[X + s][n : n + TILE], ((1,), (1,)))
                back_ref[at, s * block + n : s * block + n + TILE] = value.astype(BF)


def exchange(value):
    return lax.all_to_all(value, ("zl", "expert"), 0, 0, tiled=True)


def swap(value):
    return lax.ppermute(value, "zl", [(0, 1), (1, 0)])


def from_x(value, step):
    return lax.ppermute(value, "x", [(i, (i - step) % X) for i in range(X)]) if step else value


def weight_terms(left, right, block):
    terms = [dot(left[:, s * block : (s + 1) * block], right, ((0,), (0,))) for s in range(X)]
    return [terms[0]] + [t.astype(BF) for t in terms[1:]]


def added(terms):
    return (terms[0] + sum(from_x(t, -s).astype(F32) for s, t in enumerate(terms) if s)).astype(BF)


def moved(value, flip_mask):
    count = lax.axis_size("expert")
    bits = count.bit_length() - 1
    which = jnp.int32(0)
    for bit in range(bits):
        which = which + jnp.where(flip_mask == 1 << bit, bit, 0).astype(jnp.int32)

    def flipper(bit):
        pairs = [(i, i ^ 1 << bit) for i in range(count)]
        return lambda v: lax.ppermute(v, "expert", pairs)

    return lax.switch(which, [flipper(bit) for bit in range(bits)], value)


def shards(tokens, cotangent, expert_ids, gate_vals, partner, gate_weight, up_weight, down_weight_t):
    experts = lax.axis_size("expert")
    tok_rows, width = tokens.shape
    hidden = gate_weight.shape[2]
    block = gate_weight.shape[1]
    top = expert_ids.shape[1]
    slots = tok_rows * top
    cap = slots // experts
    part = X * block
    every = ZL * slots
    at = lax.axis_index("x").reshape(1)
    ids = expert_ids.T
    gates = gate_vals.T.astype(F32)

    def chunks(value):
        return value.reshape(ZL * experts, cap, -1)

    sent_shape = ((ZL, slots, part), BF)
    (send_rows,) = call(partial(rows_kernel, experts), [sent_shape], at, ids, tokens, scalars=1)
    (send_grads,) = call(partial(grads_kernel, experts), [sent_shape], at, ids, gates, cotangent, scalars=1)

    rows = exchange(chunks(send_rows)).reshape(every, part)
    w_gate, w_up = ([from_x(w[0], s) for s in range(X)] for w in (gate_weight, up_weight))
    send_grads, *w_pair = lax.optimization_barrier((send_grads, *w_gate, *w_up))
    grads_in = exchange(chunks(send_grads)).reshape(every, part)
    w_down = [from_x(down_weight_t[0], s) for s in range(X)]

    own, sent = call(forward_kernel, [((every, 2 * hidden), F32), ((every, 2 * hidden), BF)], rows, *w_pair, loaded=2 * X)
    pre = own + swap(sent).astype(F32)
    pre_gate, pre_up = pre[:, :hidden], pre[:, hidden:]
    sig = jax.nn.sigmoid(pre_gate)
    silu_val = pre_gate * sig
    act = (silu_val * pre_up).astype(BF)
    slope = pre_up * sig * (1.0 + pre_gate * (1.0 - sig))

    own, sent = call(forward_kernel, [((every, hidden), F32), ((every, hidden), BF)], grads_in, *w_down, loaded=X)
    down_terms = weight_terms(grads_in, act, block)
    other, *down_terms = lax.optimization_barrier((swap(sent), *down_terms))
    gate, up, back = call(
        back_kernel,
        [((every, hidden), BF), ((every, hidden), BF), ((every, part + EXTRA), BF)],
        own, other, slope, silu_val, act, *w_pair,
    )

    back = exchange(chunks(back))
    rows, down_terms[0], gate, up = lax.optimization_barrier((rows, down_terms[0], gate, up))
    flip_mask = partner[0]
    grad_down = moved(added(down_terms), flip_mask)
    grad_gate = moved(added(weight_terms(rows, gate, block)), flip_mask)
    grad_up = moved(added(weight_terms(rows, up, block)), flip_mask)
    grad_tokens, grad_gates = call(
        partial(collect_kernel, experts),
        [((tok_rows, width), BF), ((top, tok_rows), F32)],
        at, ids, gates, back.reshape(ZL, slots, part + EXTRA), scalars=1,
    )
    return grad_tokens, grad_gates.T.astype(BF), grad_gate[None], grad_up[None], grad_down[None]


def solution(mesh):
    split = Mesh(mesh.devices.reshape(X, ZL, -1), ("x", "zl", "expert"))
    every = ("x", "zl", "expert")
    tok = P(every, None)
    weight = P("expert", ("x", "zl"), None)
    return jax.shard_map(
        shards,
        mesh=split,
        in_specs=(tok, tok, tok, tok, P(), weight, weight, weight),
        out_specs=(tok, tok, weight, weight, weight),
        check_vma=False,
    )
```

```python
from functools import partial

import jax
import jax.numpy as jnp
from jax import lax
from jax.experimental import pallas as pl
from jax.experimental.pallas import tpu as pltpu
from jax.sharding import Mesh, PartitionSpec as P

BF, F32 = jnp.bfloat16, jnp.float32
X, ZL = 4, 2
EXTRA = 128
TILE = 256


def dot(a, b, dims=((1,), (0,))):
    return lax.dot_general(a, b, (dims, ((), ())), preferred_element_type=F32)


def call(kernel, outs, *args, scalars=0, loaded=0):
    spaces = [pltpu.SMEM] * scalars + [pltpu.VMEM] * (len(args) - scalars - loaded) + [pl.ANY] * loaded
    scratch = []
    if loaded:
        scratch = [pltpu.VMEM((loaded, *args[-1].shape), args[-1].dtype), pltpu.SemaphoreType.DMA((loaded,))]
    return pl.pallas_call(
        kernel,
        out_shape=[jax.ShapeDtypeStruct(shape, dtype) for shape, dtype in outs],
        in_specs=[pl.BlockSpec(memory_space=space) for space in spaces],
        out_specs=[pl.BlockSpec(memory_space=pltpu.VMEM)] * len(outs),
        scratch_shapes=scratch,
        compiler_params=pltpu.CompilerParams(vmem_limit_bytes=32 << 20),
    )(*args)


def picks_of(experts, ids):
    top, tok_rows = ids.shape
    slots = top * tok_rows
    cap = slots // experts
    expert = lax.broadcasted_iota(jnp.int32, (experts, tok_rows), 0)
    before = lax.broadcasted_iota(jnp.int32, (tok_rows, tok_rows), 0)
    before = (before < lax.broadcasted_iota(jnp.int32, (tok_rows, tok_rows), 1)).astype(BF)
    place = lax.broadcasted_iota(jnp.int32, (slots, tok_rows), 0)
    taken = jnp.zeros((experts, 1), F32)
    picks = []
    for k in range(top):
        named = expert == ids[k : k + 1]
        ones = jnp.where(named, 1.0, 0.0)
        rank = jnp.sum(jnp.where(named, dot(ones.astype(BF), before) + taken, 0.0), axis=0, keepdims=True)
        taken = taken + jnp.sum(ones, axis=1, keepdims=True)
        picks.append(place == ids[k : k + 1] * cap + rank.astype(jnp.int32))
    return picks


def gathered(picks, at, source_ref, block, scale, store):
    pick = jnp.where(picks[0] | picks[1], 1.0, 0.0).astype(BF)
    for z in range(ZL):
        for s in range(X):
            column = pl.multiple_of((lax.rem(at + s, X) * ZL + z) * block, block)
            value = dot(pick, source_ref[:, pl.ds(column, block)])
            store(z, s, (value if scale is None else value * scale).astype(BF))


def rows_kernel(experts, at_ref, ids_ref, tokens_ref, out_ref):
    block = tokens_ref.shape[1] // (X * ZL)
    picks = picks_of(experts, ids_ref[...])

    def store(z, s, value):
        out_ref[z, :, s * block : (s + 1) * block] = value

    gathered(picks, at_ref[0], tokens_ref, block, None, store)


def grads_kernel(experts, at_ref, ids_ref, gates_ref, cotangent_ref, out_ref):
    block = cotangent_ref.shape[1] // (X * ZL)
    picks = picks_of(experts, ids_ref[...])
    scale = sum(jnp.sum(jnp.where(p, gates_ref[k : k + 1], 0.0), axis=1, keepdims=True) for k, p in enumerate(picks))

    def store(z, s, value):
        out_ref[z, :, s * block : (s + 1) * block] = value

    gathered(picks, at_ref[0], cotangent_ref, block, scale, store)


def collect_kernel(experts, at_ref, ids_ref, gates_ref, back_ref, down_ref, gate_ref, tokens_ref, gates_out_ref, *copies):
    block = tokens_ref.shape[1] // (X * ZL)
    picks = picks_of(experts, ids_ref[...])
    pick = jnp.where(picks[0] | picks[1], 1.0, 0.0).astype(BF)
    for z in range(ZL):
        for s in range(X):
            column = pl.multiple_of((lax.rem(at_ref[0] + s, X) * ZL + z) * block, block)
            value = dot(pick, back_ref[z, :, s * block : (s + 1) * block], ((0,), (0,)))
            tokens_ref[:, pl.ds(column, block)] = value.astype(BF)
    total = jnp.sum(back_ref[0, :, X * block :].astype(F32), axis=1, keepdims=True)
    sums = [jnp.sum(jnp.where(p, total, 0.0), axis=0, keepdims=True) for p in picks]
    gates_out_ref[...] = jnp.concatenate(sums, axis=0) / gates_ref[...]
    copies[0][...] = down_ref[...]
    copies[1][...] = gate_ref[...]


def forward_kernel(rows_ref, *refs):
    *sources, own_ref, sent_ref, weights, sems = refs
    rows, columns = own_ref.shape
    count, block, hidden = weights.shape
    copies = [pltpu.make_async_copy(sources[i], weights.at[i], sems.at[i]) for i in range(count)]
    for copy in copies:
        copy.start()
    for i in range(count // X):
        for copy in copies[i * X : (i + 1) * X]:
            copy.wait()
        for m in range(0, rows, TILE):
            for n in range(0, hidden, TILE):
                total = None
                for s in range(X):
                    weight = weights[i * X + s, :, n : n + TILE]
                    term = dot(rows_ref[m : m + TILE, s * block : (s + 1) * block], weight)
                    total = term if total is None else total + term
                at = i * hidden + n
                own_ref[m : m + TILE, at : at + TILE] = total
                sent_ref[m : m + TILE, at : at + TILE] = total.astype(BF)


def back_kernel(own_ref, other_ref, slope_ref, silu_ref, act_ref, *refs):
    *weights, gate_ref, up_ref, back_ref = refs
    rows, hidden = own_ref.shape
    block = weights[0].shape[0]
    for m in range(0, rows, TILE):
        at = slice(m, m + TILE)
        grad_act = own_ref[at] + other_ref[at].astype(F32)
        gate_ref[at] = (grad_act * slope_ref[at]).astype(BF)
        up_ref[at] = (grad_act * silu_ref[at]).astype(BF)
        scaled = jnp.sum(act_ref[at].astype(F32) * grad_act, axis=1, keepdims=True)
        high = scaled.astype(BF).astype(F32)
        lane = lax.broadcasted_iota(jnp.int32, (TILE, EXTRA), 1)
        extra = jnp.where(lane == 0, high, jnp.where(lane == 1, scaled - high, 0.0))
        back_ref[at, X * block :] = extra.astype(BF)
        for s in range(X):
            for n in range(0, block, TILE):
                value = dot(gate_ref[at], weights[s][n : n + TILE], ((1,), (1,)))
                value = value + dot(up_ref[at], weights[X + s][n : n + TILE], ((1,), (1,)))
                back_ref[at, s * block + n : s * block + n + TILE] = value.astype(BF)


def exchange(value):
    return lax.all_to_all(value, ("zl", "expert"), 0, 0, tiled=True)


def swap(value):
    return lax.ppermute(value, "zl", [(0, 1), (1, 0)])


def from_x(value, step):
    return lax.ppermute(value, "x", [(i, (i - step) % X) for i in range(X)]) if step else value


def weight_terms(left, right, block):
    terms = [dot(left[:, s * block : (s + 1) * block], right, ((0,), (0,))) for s in range(X)]
    return [terms[0]] + [t.astype(BF) for t in terms[1:]]


def added(terms):
    return (terms[0] + sum(from_x(t, -s).astype(F32) for s, t in enumerate(terms) if s)).astype(BF)


def moved(flip_mask, *values):
    count = lax.axis_size("expert")
    bits = count.bit_length() - 1
    which = jnp.int32(0)
    for bit in range(bits):
        which = which + jnp.where(flip_mask == 1 << bit, bit, 0).astype(jnp.int32)

    def flipper(bit):
        pairs = [(i, i ^ 1 << bit) for i in range(count)]
        return lambda *v: [lax.ppermute(a, "expert", pairs) for a in v]

    return lax.switch(which, [flipper(bit) for bit in range(bits)], *values)


def shards(tokens, cotangent, expert_ids, gate_vals, partner, gate_weight, up_weight, down_weight_t):
    experts = lax.axis_size("expert")
    tok_rows, width = tokens.shape
    hidden = gate_weight.shape[2]
    block = gate_weight.shape[1]
    top = expert_ids.shape[1]
    slots = tok_rows * top
    cap = slots // experts
    part = X * block
    every = ZL * slots
    at = lax.axis_index("x").reshape(1)
    ids = expert_ids.T
    gates = gate_vals.T.astype(F32)

    def chunks(value):
        return value.reshape(ZL * experts, cap, -1)

    sent_shape = ((ZL, slots, part), BF)
    (send_rows,) = call(partial(rows_kernel, experts), [sent_shape], at, ids, tokens, scalars=1)
    (send_grads,) = call(partial(grads_kernel, experts), [sent_shape], at, ids, gates, cotangent, scalars=1)

    rows = exchange(chunks(send_rows)).reshape(every, part)
    w_gate, w_up = ([from_x(w[0], s) for s in range(X)] for w in (gate_weight, up_weight))
    send_grads, *w_pair = lax.optimization_barrier((send_grads, *w_gate, *w_up))
    grads_in = exchange(chunks(send_grads)).reshape(every, part)
    w_down = [from_x(down_weight_t[0], s) for s in range(X)]

    own, sent = call(forward_kernel, [((every, 2 * hidden), F32), ((every, 2 * hidden), BF)], rows, *w_pair, loaded=2 * X)
    pre = own + swap(sent).astype(F32)
    pre_gate, pre_up = pre[:, :hidden], pre[:, hidden:]
    sig = jax.nn.sigmoid(pre_gate)
    silu_val = pre_gate * sig
    act = (silu_val * pre_up).astype(BF)
    slope = pre_up * sig * (1.0 + pre_gate * (1.0 - sig))

    own, sent = call(forward_kernel, [((every, hidden), F32), ((every, hidden), BF)], grads_in, *w_down, loaded=X)
    down_terms = weight_terms(grads_in, act, block)
    other, *down_terms = lax.optimization_barrier((swap(sent), *down_terms))
    gate, up, back = call(
        back_kernel,
        [((every, hidden), BF), ((every, hidden), BF), ((every, part + EXTRA), BF)],
        own, other, slope, silu_val, act, *w_pair,
    )

    back = exchange(chunks(back))
    flip_mask = partner[0]
    grad_down, grad_gate = added(down_terms), added(weight_terms(rows, gate, block))
    rows, grad_down = lax.optimization_barrier((rows, grad_down))
    grad_up = added(weight_terms(rows, up, block))
    grad_down, grad_gate = moved(flip_mask, grad_down, grad_gate)
    grad_tokens, grad_gates, grad_down, grad_gate = call(
        partial(collect_kernel, experts),
        [((tok_rows, width), BF), ((top, tok_rows), F32), ((block, hidden), BF), ((block, hidden), BF)],
        at, ids, gates, back.reshape(ZL, slots, part + EXTRA), grad_down, grad_gate, scalars=1,
    )
    grad_up, grad_tokens = lax.optimization_barrier((grad_up, grad_tokens))
    (grad_up,) = moved(flip_mask, grad_up)
    return grad_tokens, grad_gates.T.astype(BF), grad_gate[None], grad_up[None], grad_down[None]


def solution(mesh):
    split = Mesh(mesh.devices.reshape(X, ZL, -1), ("x", "zl", "expert"))
    every = ("x", "zl", "expert")
    tok = P(every, None)
    weight = P("expert", ("x", "zl"), None)
    return jax.shard_map(
        shards,
        mesh=split,
        in_specs=(tok, tok, tok, tok, P(), weight, weight, weight),
        out_specs=(tok, tok, weight, weight, weight),
        check_vma=False,
    )
```

```python
from functools import partial

import jax
import jax.numpy as jnp
from jax import lax
from jax.experimental import pallas as pl
from jax.experimental.pallas import tpu as pltpu
from jax.sharding import Mesh, PartitionSpec as P

BF, F32 = jnp.bfloat16, jnp.float32
X, ZL = 4, 2
EXTRA = 128
TILE = 256


def dot(a, b, dims=((1,), (0,))):
    return lax.dot_general(a, b, (dims, ((), ())), preferred_element_type=F32)


def call(kernel, outs, *args, scalars=0, loaded=0):
    spaces = [pltpu.SMEM] * scalars + [pltpu.VMEM] * (len(args) - scalars - loaded) + [pl.ANY] * loaded
    scratch = []
    if loaded:
        scratch = [pltpu.VMEM((loaded, *args[-1].shape), args[-1].dtype), pltpu.SemaphoreType.DMA((loaded,))]
    return pl.pallas_call(
        kernel,
        out_shape=[jax.ShapeDtypeStruct(shape, dtype) for shape, dtype in outs],
        in_specs=[pl.BlockSpec(memory_space=space) for space in spaces],
        out_specs=[pl.BlockSpec(memory_space=pltpu.VMEM)] * len(outs),
        scratch_shapes=scratch,
        compiler_params=pltpu.CompilerParams(vmem_limit_bytes=(56 if loaded else 32) << 20),
    )(*args)


def picks_of(experts, ids):
    top, tok_rows = ids.shape
    slots = top * tok_rows
    cap = slots // experts
    expert = lax.broadcasted_iota(jnp.int32, (experts, tok_rows), 0)
    before = lax.broadcasted_iota(jnp.int32, (tok_rows, tok_rows), 0)
    before = (before < lax.broadcasted_iota(jnp.int32, (tok_rows, tok_rows), 1)).astype(BF)
    place = lax.broadcasted_iota(jnp.int32, (slots, tok_rows), 0)
    taken = jnp.zeros((experts, 1), F32)
    picks = []
    for k in range(top):
        named = expert == ids[k : k + 1]
        ones = jnp.where(named, 1.0, 0.0)
        rank = jnp.sum(jnp.where(named, dot(ones.astype(BF), before) + taken, 0.0), axis=0, keepdims=True)
        taken = taken + jnp.sum(ones, axis=1, keepdims=True)
        picks.append(place == ids[k : k + 1] * cap + rank.astype(jnp.int32))
    return picks


def gathered(picks, at, source_ref, block, scale, store):
    pick = jnp.where(picks[0] | picks[1], 1.0, 0.0).astype(BF)
    for z in range(ZL):
        for s in range(X):
            column = pl.multiple_of((lax.rem(at + s, X) * ZL + z) * block, block)
            value = dot(pick, source_ref[:, pl.ds(column, block)])
            store(z, s, (value if scale is None else value * scale).astype(BF))


def rows_kernel(experts, at_ref, ids_ref, tokens_ref, out_ref):
    block = tokens_ref.shape[1] // (X * ZL)
    picks = picks_of(experts, ids_ref[...])

    def store(z, s, value):
        out_ref[z, :, s * block : (s + 1) * block] = value

    gathered(picks, at_ref[0], tokens_ref, block, None, store)


def grads_kernel(experts, at_ref, ids_ref, gates_ref, cotangent_ref, out_ref):
    block = cotangent_ref.shape[1] // (X * ZL)
    picks = picks_of(experts, ids_ref[...])
    scale = sum(jnp.sum(jnp.where(p, gates_ref[k : k + 1], 0.0), axis=1, keepdims=True) for k, p in enumerate(picks))

    def store(z, s, value):
        out_ref[z, :, s * block : (s + 1) * block] = value

    gathered(picks, at_ref[0], cotangent_ref, block, scale, store)


def collect_kernel(experts, at_ref, ids_ref, gates_ref, back_ref, down_ref, gate_ref, tokens_ref, gates_out_ref, *copies):
    block = tokens_ref.shape[1] // (X * ZL)
    picks = picks_of(experts, ids_ref[...])
    pick = jnp.where(picks[0] | picks[1], 1.0, 0.0).astype(BF)
    for z in range(ZL):
        for s in range(X):
            column = pl.multiple_of((lax.rem(at_ref[0] + s, X) * ZL + z) * block, block)
            value = dot(pick, back_ref[z, :, s * block : (s + 1) * block], ((0,), (0,)))
            tokens_ref[:, pl.ds(column, block)] = value.astype(BF)
    total = jnp.sum(back_ref[0, :, X * block :].astype(F32), axis=1, keepdims=True)
    sums = [jnp.sum(jnp.where(p, total, 0.0), axis=0, keepdims=True) for p in picks]
    gates_out_ref[...] = jnp.concatenate(sums, axis=0) / gates_ref[...]
    copies[0][...] = down_ref[...]
    copies[1][...] = gate_ref[...]


def forward_kernel(rows_ref, *refs):
    *sources, own_ref, sent_ref, weights, sems = refs
    rows, columns = own_ref.shape
    count, block, hidden = weights.shape
    copies = [pltpu.make_async_copy(sources[i], weights.at[i], sems.at[i]) for i in range(count)]
    for copy in copies:
        copy.start()
    for i in range(count // X):
        for copy in copies[i * X : (i + 1) * X]:
            copy.wait()
        for m in range(0, rows, TILE):
            for n in range(0, hidden, TILE):
                total = None
                for s in range(X):
                    weight = weights[i * X + s, :, n : n + TILE]
                    term = dot(rows_ref[m : m + TILE, s * block : (s + 1) * block], weight)
                    total = term if total is None else total + term
                at = i * hidden + n
                own_ref[m : m + TILE, at : at + TILE] = total
                sent_ref[m : m + TILE, at : at + TILE] = total.astype(BF)


def back_kernel(own_ref, other_ref, slope_ref, silu_ref, act_ref, *refs):
    *weights, gate_ref, up_ref, back_ref = refs
    rows, hidden = own_ref.shape
    block = weights[0].shape[0]
    for m in range(0, rows, TILE):
        at = slice(m, m + TILE)
        grad_act = own_ref[at] + other_ref[at].astype(F32)
        gate_ref[at] = (grad_act * slope_ref[at]).astype(BF)
        up_ref[at] = (grad_act * silu_ref[at]).astype(BF)
        scaled = jnp.sum(act_ref[at].astype(F32) * grad_act, axis=1, keepdims=True)
        high = scaled.astype(BF).astype(F32)
        lane = lax.broadcasted_iota(jnp.int32, (TILE, EXTRA), 1)
        extra = jnp.where(lane == 0, high, jnp.where(lane == 1, scaled - high, 0.0))
        back_ref[at, X * block :] = extra.astype(BF)
        for s in range(X):
            for n in range(0, block, TILE):
                value = dot(gate_ref[at], weights[s][n : n + TILE], ((1,), (1,)))
                value = value + dot(up_ref[at], weights[X + s][n : n + TILE], ((1,), (1,)))
                back_ref[at, s * block + n : s * block + n + TILE] = value.astype(BF)


def exchange(value):
    return lax.all_to_all(value, ("zl", "expert"), 0, 0, tiled=True)


def swap(value):
    return lax.ppermute(value, "zl", [(0, 1), (1, 0)])


def from_x(value, step):
    return lax.ppermute(value, "x", [(i, (i - step) % X) for i in range(X)]) if step else value


def weight_terms(left, right, block):
    terms = [dot(left[:, s * block : (s + 1) * block], right, ((0,), (0,))) for s in range(X)]
    return [terms[0]] + [t.astype(BF) for t in terms[1:]]


def added(terms):
    return (terms[0] + sum(from_x(t, -s).astype(F32) for s, t in enumerate(terms) if s)).astype(BF)


def moved(flip_mask, *values):
    count = lax.axis_size("expert")
    bits = count.bit_length() - 1
    which = jnp.int32(0)
    for bit in range(bits):
        which = which + jnp.where(flip_mask == 1 << bit, bit, 0).astype(jnp.int32)

    def flipper(bit):
        pairs = [(i, i ^ 1 << bit) for i in range(count)]
        return lambda *v: [lax.ppermute(a, "expert", pairs) for a in v]

    return lax.switch(which, [flipper(bit) for bit in range(bits)], *values)


def shards(tokens, cotangent, expert_ids, gate_vals, partner, gate_weight, up_weight, down_weight_t):
    experts = lax.axis_size("expert")
    tok_rows, width = tokens.shape
    hidden = gate_weight.shape[2]
    block = gate_weight.shape[1]
    top = expert_ids.shape[1]
    slots = tok_rows * top
    cap = slots // experts
    part = X * block
    every = ZL * slots
    at = lax.axis_index("x").reshape(1)
    ids = expert_ids.T
    gates = gate_vals.T.astype(F32)

    def chunks(value):
        return value.reshape(ZL * experts, cap, -1)

    sent_shape = ((ZL, slots, part), BF)
    (send_rows,) = call(partial(rows_kernel, experts), [sent_shape], at, ids, tokens, scalars=1)
    (send_grads,) = call(partial(grads_kernel, experts), [sent_shape], at, ids, gates, cotangent, scalars=1)

    rows = exchange(chunks(send_rows)).reshape(every, part)
    w_gate, w_up = ([from_x(w[0], s) for s in range(X)] for w in (gate_weight, up_weight))
    send_grads, *w_pair = lax.optimization_barrier((send_grads, *w_gate, *w_up))
    grads_in = exchange(chunks(send_grads)).reshape(every, part)
    w_down = [from_x(down_weight_t[0], s) for s in range(X)]

    own, sent = call(forward_kernel, [((every, 2 * hidden), F32), ((every, 2 * hidden), BF)], rows, *w_pair, loaded=2 * X)
    pre = own + swap(sent).astype(F32)
    pre_gate, pre_up = pre[:, :hidden], pre[:, hidden:]
    sig = jax.nn.sigmoid(pre_gate)
    silu_val = pre_gate * sig
    act = (silu_val * pre_up).astype(BF)
    slope = pre_up * sig * (1.0 + pre_gate * (1.0 - sig))

    own, sent = call(forward_kernel, [((every, hidden), F32), ((every, hidden), BF)], grads_in, *w_down, loaded=X)
    down_terms = weight_terms(grads_in, act, block)
    other, *down_terms = lax.optimization_barrier((swap(sent), *down_terms))
    gate, up, back = call(
        back_kernel,
        [((every, hidden), BF), ((every, hidden), BF), ((every, part + EXTRA), BF)],
        own, other, slope, silu_val, act, *w_pair,
    )

    back = exchange(chunks(back))
    flip_mask = partner[0]
    grad_down, grad_gate = added(down_terms), added(weight_terms(rows, gate, block))
    rows, grad_down = lax.optimization_barrier((rows, grad_down))
    grad_up = added(weight_terms(rows, up, block))
    grad_down, grad_gate = moved(flip_mask, grad_down, grad_gate)
    grad_tokens, grad_gates, grad_down, grad_gate = call(
        partial(collect_kernel, experts),
        [((tok_rows, width), BF), ((top, tok_rows), F32), ((block, hidden), BF), ((block, hidden), BF)],
        at, ids, gates, back.reshape(ZL, slots, part + EXTRA), grad_down, grad_gate, scalars=1,
    )
    grad_up, grad_tokens = lax.optimization_barrier((grad_up, grad_tokens))
    (grad_up,) = moved(flip_mask, grad_up)
    return grad_tokens, grad_gates.T.astype(BF), grad_gate[None], grad_up[None], grad_down[None]


def solution(mesh):
    split = Mesh(mesh.devices.reshape(X, ZL, -1), ("x", "zl", "expert"))
    every = ("x", "zl", "expert")
    tok = P(every, None)
    weight = P("expert", ("x", "zl"), None)
    return jax.shard_map(
        shards,
        mesh=split,
        in_specs=(tok, tok, tok, tok, P(), weight, weight, weight),
        out_specs=(tok, tok, weight, weight, weight),
        check_vma=False,
    )
```
